32 devices in a mesh: col: 8 (over z, x), sec: 4 (over y, core).
Axes of the slice: x: 2, y: 2, z: 4, core: 2. Of those that a mesh axis runs over, the one named last changes fastest.
Arguments:
- left_start: bfloat16 [2048, 6, 1024], P('sec'), may hold values from -6 to 6
- coupling: bfloat16 [8, 2048, 2304], P('col', 'sec'), may hold values from -0.125 to 0.125
- tensor: float32 [8, 6, 6, 6, 6], P('col'), may hold values from -1 to 1
- sketch: float32 [8, 6, 1024], P('col'), may hold values from -3 to 3
- block_parity: int32 [16], replicated, may hold values from 0 to 1
- leg_parity: int32 [8, 6], replicated, may hold values from 0 to 1, as said below
Outputs:
- states: bfloat16 [8, 2048, 6, 1024], P('col', 'sec')
- grams: float32 [8, 1024, 1024], P('col', 'sec')
The draws below stay inside these ranges and needn't reach their ends.
Inputs may be any that keep to these rules, and one draw needn't show every extreme that they name: `leg_parity`: in each column exactly half of the 6 leg states are odd.
All inputs are finite; a program needn't handle non-finite values.
Results may differ from the reference program's by a relative error of at most 0.019.
Values may be sent and summed in bfloat16 or wider, within the bound.
No kernel may reach another device: no remote copies, remote signals or barrier semaphores. Data moves between devices by JAX's collectives and lax.ppermute only.
A program may use at most 192 MiB of HBM per device.

```python
import jax
import jax.numpy as jnp
from jax import lax

CHI = 2048
D = 6
K = 1024
PAN = 128
NPAN = 16
N_COL = 8


def draw_leg_parity(key, part):
    halves = (jnp.arange(D) % 2).astype(jnp.int32)
    row_keys = jax.random.split(jax.random.fold_in(key, 11), N_COL)
    return jax.vmap(lambda row_key: jax.random.permutation(row_key, halves))(row_keys)


def draw_left_start(key, part):
    values = jnp.clip(jax.random.normal(jax.random.fold_in(key, 21), (CHI, D, K), jnp.float32), -6.0, 6.0)
    return values.astype(jnp.bfloat16)


def draw_sketch(key, part):
    raw = jax.random.normal(jax.random.fold_in(key, 31), (N_COL, D, K), jnp.float32)
    spread = jnp.sqrt(jnp.maximum(jnp.mean(raw * raw, axis=1, keepdims=True), 0.05))
    return jnp.clip(raw / spread, -2.4, 2.4)


def touch_ends(entries, rng, smallest, largest):
    extent = entries.shape
    place = [jax.random.randint(jax.random.fold_in(rng, axis), (), 0, extent[axis]) for axis in range(len(extent))]
    entries = entries.at[tuple(place)].set(smallest)
    longest = extent.index(max(extent))
    place[longest] = (place[longest] + 1) % extent[longest]
    return entries.at[tuple(place)].set(largest)


def block_levels(stream_key, dims, cuts, smallest, largest):
    def one(axis_at, shards_of):
        steps = jax.random.uniform(jax.random.fold_in(jax.random.fold_in(stream_key, 6), axis_at), (shards_of,), jnp.float32, smallest / len(cuts), largest / len(cuts))
        return jnp.repeat(jnp.exp(steps), dims[axis_at] // shards_of).reshape((-1,) + (1,) * (len(dims) - axis_at - 1))

    gain = one(*cuts[0])
    for cut in cuts[1:]:
        gain = gain * one(*cut)
    return gain


def scatter_about(own_key, dims, scale, most, cuts=(), held_as=jnp.bfloat16):
    factor_of = block_levels(own_key, dims, cuts, -0.22, 0.18) if cuts else 1.0
    entries = jax.random.normal(own_key, dims, jnp.float32) * scale * factor_of
    return jnp.minimum(jnp.maximum(entries, -most), most).astype(held_as)


def setup_inputs(seed: int = 0) -> dict:
    seeds = jax.random.split(jax.random.key(seed), 7)
    left_start = draw_left_start(jax.random.fold_in(seeds[6], 71), 0)
    coupling = scatter_about(seeds[1], (N_COL, CHI, 3 * PAN * D), (3 * PAN * D) ** -0.5, 0.125, ((0, 8), (1, 4)))
    tensor = scatter_about(seeds[2], (N_COL, D, D, D, D), (D * D) ** -0.5, 1.0, ((0, 8),), jnp.float32)
    sketch = draw_sketch(jax.random.fold_in(seeds[6], 71), 0)
    block_parity = touch_ends(jax.random.randint(seeds[4], (NPAN,), 0, 2), jax.random.fold_in(seeds[4], 1), 0, 1).astype(jnp.int32)
    leg_parity = draw_leg_parity(jax.random.fold_in(seeds[6], 71), 0)
    return dict(left_start=left_start, coupling=coupling, tensor=tensor, sketch=sketch, block_parity=block_parity, leg_parity=leg_parity)


def reference(left_start, coupling, tensor, sketch, block_parity, leg_parity):
    panel_count = CHI // PAN
    carried = left_start
    sketch_list = []
    gram_list = []
    for column in range(N_COL):
        odd_pairs = block_parity.astype(jnp.float32)[:, None] * leg_parity[column].astype(jnp.float32)[None, :]
        sign_table = jnp.repeat(1.0 - 2.0 * odd_pairs, PAN, axis=0)
        mixing = jnp.einsum("duez,zk->duek", tensor[column], sketch[column], precision=lax.Precision.HIGHEST)
        weighted = jnp.einsum("adk,duek->auek", carried.astype(jnp.float32), mixing, precision=lax.Precision.HIGHEST)
        weighted = (weighted * sign_table[:, :, None, None]).astype(jnp.bfloat16)
        flattened = weighted.reshape(CHI * D, D * K)
        padded = jnp.pad(flattened, ((PAN * D, PAN * D), (0, 0)))
        pieces = []
        for panel in range(panel_count):
            window = padded[panel * PAN * D:(panel + 3) * PAN * D]
            band_rows = coupling[column, panel * PAN:(panel + 1) * PAN]
            pieces.append(jnp.dot(band_rows, window, preferred_element_type=jnp.float32))
        carried = jnp.concatenate(pieces, 0).astype(jnp.bfloat16).reshape(CHI, D, K)
        flat_state = carried.reshape(CHI * D, K)
        gram_now = jnp.dot(flat_state.T, flat_state, preferred_element_type=jnp.float32) / (CHI * D)
        sketch_list.append(carried)
        gram_list.append(gram_now)
    return jnp.stack(sketch_list), jnp.stack(gram_list)
```

```python
import functools

import jax
import jax.numpy as jnp
from jax import lax
from jax.experimental import pallas as pl
from jax.experimental.pallas import tpu as pltpu
from jax.sharding import PartitionSpec as P

CHI = 2048
D = 6
PAN = 128
KB = 64
PAIRS = D // 2
LANES = PAIRS * 2 * KB
STACK = D * PAN
BAND = 3 * PAN
TERMS = D * PAIRS * D
MIB = 1024 * 1024


def ordering_matrix():
    row = lax.broadcasted_iota(jnp.int32, (STACK, STACK), 0)
    col = lax.broadcasted_iota(jnp.int32, (STACK, STACK), 1)
    return (col == (row % D) * PAN + row // D).astype(jnp.bfloat16)


def order_kernel(sign_ref, band_ref, perm_ref, out_ref):
    p, w = pl.program_id(0), pl.program_id(1)
    moved = jnp.dot(band_ref[...], perm_ref[...], preferred_element_type=jnp.float32)
    for u in range(D):
        part = moved[:, u * PAN : (u + 1) * PAN] * sign_ref[p, w * D + u]
        out_ref[0, u * PAN : (u + 1) * PAN, :] = part.astype(jnp.bfloat16)


def ordered_coupling(coupling, signs):
    rows = coupling.shape[0]
    panels = rows // PAN
    return pl.pallas_call(
        order_kernel,
        grid=(panels, 3),
        in_specs=[
            pl.BlockSpec(memory_space=pltpu.SMEM),
            pl.BlockSpec((PAN, STACK), lambda p, w: (p, w)),
            pl.BlockSpec((STACK, STACK), lambda p, w: (0, 0)),
        ],
        out_specs=pl.BlockSpec((1, STACK, PAN), lambda p, w: (p, 0, w)),
        out_shape=jax.ShapeDtypeStruct((panels, STACK, BAND), jnp.bfloat16),
        compiler_params=pltpu.CompilerParams(vmem_limit_bytes=32 * MIB),
        name="order_coupling",
    )(signs, coupling, ordering_matrix())


def mix_rows(y_ref, mix_ref, column, res_ref):
    lane = lax.broadcasted_iota(jnp.int32, (4, 8, 2 * KB), 2)
    low = lane < KB
    for chunk in range(PAN // 32):
        start = chunk * 32
        acc = [None] * D
        for u in range(D):
            for q in range(PAIRS):
                y = y_ref[u * PAN + start : u * PAN + start + 32, q * 128 : (q + 1) * 128]
                y = y.reshape(4, 8, 128)
                for e in range(D):
                    term = y * mix_ref[column, (u * PAIRS + q) * D + e][None]
                    acc[e] = term if acc[e] is None else acc[e] + term
        for q in range(PAIRS):
            even, odd = acc[2 * q], acc[2 * q + 1]
            even = even + pltpu.roll(even.reshape(32, 128), KB, 1).reshape(4, 8, 128)
            odd = odd + pltpu.roll(odd.reshape(32, 128), KB, 1).reshape(4, 8, 128)
            both = jnp.where(low, even, odd).reshape(32, 128)
            res_ref[start : start + 32, q * 128 : (q + 1) * 128] = both.astype(jnp.bfloat16)


def turn_kernel(
    panels, odd_first, count,
    flag_ref, left_ref, low_ref, mid_ref, high_ref, ca_ref, cb_ref, mix_ref,
    keep_ref, send_ref, pass_ref,
    src, ya, yb, wide, res_a, res_b,
):
    s = pl.program_id(0)
    is_odd_home = flag_ref[0]
    is_first = flag_ref[1]
    even_total = panels + 2
    dump = 2 * panels + 6

    @pl.when(s == 0)
    def _():
        @pl.when(is_first == 1)
        def _():
            src[0 : panels + 4] = left_ref[0]

        @pl.when(is_first == 0)
        def _():
            src[0:2] = low_ref[...]
            src[2 : panels + 2] = mid_ref[...]
            src[panels + 2 : panels + 4] = high_ref[...]

        src[panels + 4 :] = jnp.zeros((panels + 3, PAN, LANES), jnp.bfloat16)
        yb[...] = jnp.zeros_like(yb)
        for column in range(2):
            for i in range(TERMS):
                wide[column, i] = jnp.broadcast_to(mix_ref[0, column, i : i + 1, :], (8, 128))

    def window(n):
        odd = jnp.clip(n - odd_first, 0, panels - 1) + panels + 4
        base = jnp.where(n < odd_first, jnp.minimum(n, panels + 1), odd)
        return src[pl.ds(base, 3)].reshape(BAND, LANES)

    def hand_out(n, res):
        slot = jnp.where((n >= 0) & (n < even_total), panels + 4 + n, dump)
        src[pl.ds(slot, 1)] = res[...][None]
        own_even = (n >= 1) & (n <= panels)
        own_odd = (n >= odd_first) & (n < odd_first + panels)
        to_keep = jnp.where(is_odd_home == 1, own_odd, own_even)
        to_send = jnp.where(is_odd_home == 1, own_even, own_odd)
        at_even = jnp.clip(n - 1, 0, panels - 1)
        at_odd = jnp.clip(n - odd_first, 0, panels - 1)
        at = jnp.where(own_odd, at_odd, at_even)

        @pl.when(to_keep)
        def _():
            keep_ref[pl.ds(at, 1)] = res[...][None]

        @pl.when(to_send)
        def _():
            send_ref[pl.ds(at, 1)] = res[...][None]

        @pl.when(own_odd)
        def _():
            pass_ref[pl.ds(at, 1)] = res[...][None]

    def phase(n):
        return (n >= odd_first).astype(jnp.int32)

    n = 2 * s

    @pl.when(s < count // 2)
    def _():
        ya[...] = jnp.dot(ca_ref[0], window(n), preferred_element_type=jnp.float32)
        mix_rows(yb, wide, phase(n - 1), res_b)
        hand_out(n - 1, res_b)
        yb[...] = jnp.dot(cb_ref[0], window(n + 1), preferred_element_type=jnp.float32)
        mix_rows(ya, wide, phase(n), res_a)
        hand_out(n, res_a)

    @pl.when(s == count // 2)
    def _():
        mix_rows(yb, wide, phase(n - 1), res_b)
        hand_out(n - 1, res_b)


def one_turn(flags, left, low, mid, high, bands, mixing):
    panels = mid.shape[0]
    gap = 0 if panels >= 2 else 1
    odd_first = panels + 2 + gap
    count = odd_first + panels
    count += count % 2
    last = 2 * panels + 1

    def band_at(n):
        return jnp.minimum(jnp.where(n < odd_first, jnp.minimum(n, panels + 1), n - gap), last)

    block = jax.ShapeDtypeStruct((panels, PAN, LANES), jnp.bfloat16)
    whole = lambda shape: pl.BlockSpec(shape, lambda s, f: (0,) * len(shape))
    spec = pltpu.PrefetchScalarGridSpec(
        num_scalar_prefetch=1,
        grid=(count // 2 + 1,),
        in_specs=[
            pl.BlockSpec((1, panels + 4, PAN, LANES), lambda s, f: (f[2], 0, 0, 0)),
            whole((2, PAN, LANES)),
            whole((panels, PAN, LANES)),
            whole((2, PAN, LANES)),
            pl.BlockSpec((1, STACK, BAND), lambda s, f: (band_at(2 * s), 0, 0)),
            pl.BlockSpec((1, STACK, BAND), lambda s, f: (band_at(2 * s + 1), 0, 0)),
            pl.BlockSpec((1, 2, TERMS, 128), lambda s, f: (f[2], 0, 0, 0)),
        ],
        out_specs=[whole((panels, PAN, LANES))] * 3,
        scratch_shapes=[
            pltpu.VMEM((2 * panels + 7, PAN, LANES), jnp.bfloat16),
            pltpu.VMEM((STACK, LANES), jnp.float32),
            pltpu.VMEM((STACK, LANES), jnp.float32),
            pltpu.VMEM((2, TERMS, 8, 128), jnp.float32),
            pltpu.VMEM((PAN, LANES), jnp.bfloat16),
            pltpu.VMEM((PAN, LANES), jnp.bfloat16),
        ],
    )
    steps = 2 * panels + 2
    return pl.pallas_call(
        functools.partial(turn_kernel, panels, odd_first, count),
        grid_spec=spec,
        out_shape=[block] * 3,
        compiler_params=pltpu.CompilerParams(vmem_limit_bytes=40 * MIB),
        cost_estimate=pl.CostEstimate(
            flops=steps * 2 * STACK * BAND * LANES * 2,
            bytes_accessed=steps * STACK * BAND * 2 * 3,
            transcendentals=0,
        ),
        name="two_columns",
    )(flags, left, low, mid, high, bands, bands, mixing)


def unpack_kernel(at_ref, held_ref, one_ref, two_ref, out_ref):
    rows = one_ref.shape[1]
    low = lax.broadcasted_iota(jnp.int32, (rows, 128), 1) < KB
    for q in range(PAIRS):
        one = one_ref[0, :, q * 128 : (q + 1) * 128].astype(jnp.float32)
        two = two_ref[0, :, q * 128 : (q + 1) * 128].astype(jnp.float32)
        first = jnp.where(low, one, pltpu.roll(two, KB, 1))
        second = jnp.where(low, pltpu.roll(one, KB, 1), two)
        out_ref[2 * q] = first.astype(jnp.bfloat16)
        out_ref[2 * q + 1] = second.astype(jnp.bfloat16)


def unpacked(at, held, one, two):
    panels = one.shape[0]
    return pl.pallas_call(
        unpack_kernel,
        grid_spec=pltpu.PrefetchScalarGridSpec(
            num_scalar_prefetch=1,
            grid=(panels,),
            in_specs=[
                pl.BlockSpec(memory_space=pl.ANY),
                pl.BlockSpec((1, PAN, LANES), lambda p, f: (p, 0, 0)),
                pl.BlockSpec((1, PAN, LANES), lambda p, f: (p, 0, 0)),
            ],
            out_specs=pl.BlockSpec((D, PAN, 128), lambda p, f: (0, p, f[0])),
        ),
        out_shape=jax.ShapeDtypeStruct(held.shape, held.dtype),
        input_output_aliases={1: 0},
        compiler_params=pltpu.CompilerParams(vmem_limit_bytes=32 * MIB),
        name="unpack",
    )(at, held, one, two)


def edges(block, width, axis_dim=0):
    count = lax.axis_size("sec")
    have = block.shape[axis_dim]
    low_parts, high_parts = [], []
    reach = 0
    while width > reach:
        hop = reach // have + 1
        take = min(have, width - reach)
        forward = [(i, i + hop) for i in range(count - hop)]
        backward = [(i + hop, i) for i in range(count - hop)]
        top = lax.slice_in_dim(block, have - take, have, axis=axis_dim)
        bottom = lax.slice_in_dim(block, 0, take, axis=axis_dim)
        low_parts.insert(0, lax.ppermute(top, "sec", forward))
        high_parts.append(lax.ppermute(bottom, "sec", backward))
        reach += take
    if len(low_parts) == 1:
        return low_parts[0], high_parts[0]
    return jnp.concatenate(low_parts, axis_dim), jnp.concatenate(high_parts, axis_dim)


def on_device(left_start, coupling, tensor, sketch, block_parity, leg_parity):
    row_count, _, rank = left_start.shape
    panels = row_count // PAN
    col_count = lax.axis_size("col")
    sec_count = lax.axis_size("sec")
    col_index = lax.axis_index("col")
    sec_index = lax.axis_index("sec")
    stage = col_index // 2
    half = col_index % 2
    stages = col_count // 2
    half_cols = rank // 2
    blocks = half_cols // KB
    swap = [(i, i ^ 1) for i in range(col_count)]
    up = [(i, i + 2) for i in range(col_count - 2)]

    legs = lax.dynamic_index_in_dim(leg_parity, col_index, 0, keepdims=False)
    parity = lax.dynamic_slice_in_dim(
        jnp.pad(block_parity, (1, 1)), sec_index * panels, panels + 2, 0
    )
    table = 1.0 - 2.0 * (parity[:, None] * legs[None, :]).astype(jnp.float32)
    signs = jnp.stack([table[w : w + panels] for w in range(3)], 1).reshape(panels, 3 * D)
    own = ordered_coupling(coupling[0], signs)
    other = lax.ppermute(own, "col", swap)
    own_low, own_high = edges(own, 1)
    other_low, other_high = edges(other, 1)
    odd_home = half == 1
    even_bands = [
        jnp.where(odd_home, b, a)
        for a, b in ((own_low, other_low), (own, other), (own_high, other_high))
    ]
    bands = jnp.concatenate(even_bands + [jnp.where(odd_home, own, other)], 0)

    small = jnp.concatenate([tensor[0].reshape(D, D * D * D), sketch[0]], 1)
    small_other = lax.ppermute(small, "col", swap)

    def mixing_of(both):
        legs_part = both[:, : D * D * D].reshape(D, D, D, D)
        cols = lax.dynamic_slice_in_dim(both, D * D * D + half * half_cols, half_cols, 1)
        m = jnp.einsum("duez,zk->duek", legs_part, cols, precision=lax.Precision.HIGHEST)
        m = m.reshape(PAIRS, 2, D, D, blocks, KB).transpose(4, 2, 0, 3, 1, 5)
        return m.reshape(blocks, TERMS, 2 * KB)

    mixing = jnp.stack(
        [
            mixing_of(jnp.where(odd_home, small_other, small)),
            mixing_of(jnp.where(odd_home, small, small_other)),
        ],
        1,
    )

    mine = lax.dynamic_slice_in_dim(left_start, half * half_cols, half_cols, 2)
    mine = mine.reshape(panels, PAN, PAIRS, 2, blocks, KB).transpose(4, 0, 1, 2, 3, 5)
    mine = mine.reshape(blocks, panels, PAN, LANES)
    left_low, left_high = edges(mine, 2, 1)
    left = jnp.concatenate([left_low, mine, left_high], 1)

    skew = 2
    turns = blocks + skew * (stages - 1)
    zero_edge = jnp.zeros((2, PAN, LANES), jnp.bfloat16)
    zero_mid = jnp.zeros((panels, PAN, LANES), jnp.bfloat16)
    arrived = {t: (zero_edge, zero_mid, zero_edge) for t in range(skew)}
    keeps, sends = {}, {}
    kept, got = [], []
    lag = skew * (stages - 1)
    states = jnp.zeros((D, row_count, rank), jnp.bfloat16)

    def staged(table_of, i):
        out = table_of[i + lag]
        for z in range(stages - 1):
            out = jnp.where(stage == z, table_of[i + skew * z], out)
        return out

    for t in range(turns):
        index = jnp.clip(t - skew * stage, 0, blocks - 1)
        flags = jnp.stack([half, (stage == 0).astype(jnp.int32), index]).astype(jnp.int32)
        low, mid, high = arrived.pop(t)
        keeps[t], sends[t], passed = one_turn(flags, left, low, mid, high, bands, mixing)
        if t + skew < turns:
            nxt = lax.ppermute(passed, "col", up)
            nlow, nhigh = edges(nxt, 2)
            arrived[t + skew] = (nlow, nxt, nhigh)
        if t >= lag:
            i = t - lag
            got.append(lax.ppermute(staged(sends, i), "col", swap))
            kept.append(staged(keeps, i))
            if i % 2 == 1:
                at_own = (half * (blocks // 2) + i // 2).astype(jnp.int32)[None]
                at_got = ((1 - half) * (blocks // 2) + i // 2).astype(jnp.int32)[None]
                states = unpacked(at_own, states, kept[i - 1], kept[i])
                states = unpacked(at_got, states, got[i - 1], got[i])

    flat = states.reshape(D * row_count, rank)
    partial = lax.dot_general(
        flat, flat, (((0,), (0,)), ((), ())), preferred_element_type=jnp.float32
    ).astype(jnp.bfloat16)
    share = rank // sec_count
    gram = partial.reshape(sec_count, share, rank)
    width = 1
    while width < sec_count:
        bit = (sec_index // width) % 2
        pairs = gram.reshape(-1, 2, share, rank)
        stay = lax.dynamic_index_in_dim(pairs, bit, 1, keepdims=False)
        away = lax.dynamic_index_in_dim(pairs, 1 - bit, 1, keepdims=False)
        come = lax.ppermute(away, "sec", [(i, i ^ width) for i in range(sec_count)])
        gram = stay.astype(jnp.float32) + come.astype(jnp.float32)
        if gram.shape[0] > 1:
            gram = gram.astype(jnp.bfloat16)
        width *= 2
    gram_out = gram * (1.0 / (CHI * D))
    return states.transpose(1, 0, 2)[None], gram_out


def solution(mesh):
    in_specs = (
        P("sec", None, None),
        P("col", "sec", None),
        P("col", None, None, None, None),
        P("col", None, None),
        P(),
        P(),
    )
    out_specs = (P("col", "sec", None, None), P("col", "sec", None))
    return jax.shard_map(
        on_device, mesh=mesh, in_specs=in_specs, out_specs=out_specs, check_vma=False
    )
```

```python
import functools

import jax
import jax.numpy as jnp
from jax import lax
from jax.experimental import pallas as pl
from jax.experimental.pallas import tpu as pltpu
from jax.sharding import PartitionSpec as P

CHI = 2048
D = 6
PAN = 128
KB = 64
PAIRS = D // 2
LANES = PAIRS * 2 * KB
STACK = D * PAN
BAND = 3 * PAN
TERMS = D * PAIRS * D
ROWS = 32
SPLIT = 2
SKEW = 2
MIB = 1024 * 1024


def ordering_matrix():
    row = lax.broadcasted_iota(jnp.int32, (STACK, STACK), 0)
    col = lax.broadcasted_iota(jnp.int32, (STACK, STACK), 1)
    return (col == (row % D) * PAN + row // D).astype(jnp.bfloat16)


def order_kernel(sign_ref, band_ref, perm_ref, out_ref):
    p, w = pl.program_id(0), pl.program_id(1)
    moved = jnp.dot(band_ref[...], perm_ref[...], preferred_element_type=jnp.float32)
    for u in range(D):
        part = moved[:, u * PAN : (u + 1) * PAN] * sign_ref[p, w * D + u]
        out_ref[0, u * PAN : (u + 1) * PAN, :] = part.astype(jnp.bfloat16)


def ordered_coupling(coupling, signs):
    rows = coupling.shape[0]
    panels = rows // PAN
    return pl.pallas_call(
        order_kernel,
        grid=(panels, 3),
        in_specs=[
            pl.BlockSpec(memory_space=pltpu.SMEM),
            pl.BlockSpec((PAN, STACK), lambda p, w: (p, w)),
            pl.BlockSpec((STACK, STACK), lambda p, w: (0, 0)),
        ],
        out_specs=pl.BlockSpec((1, STACK, PAN), lambda p, w: (p, 0, w)),
        out_shape=jax.ShapeDtypeStruct((panels, STACK, BAND), jnp.bfloat16),
        compiler_params=pltpu.CompilerParams(vmem_limit_bytes=32 * MIB),
        name="order_coupling",
    )(signs, coupling, ordering_matrix())


def mix_rows(y_ref, mix_ref, column, res_ref, starts):
    low = lax.broadcasted_iota(jnp.int32, (ROWS, 2 * KB), 1) < KB
    for start in starts:
        acc = [None] * D
        for u in range(D):
            for q in range(PAIRS):
                y = y_ref[u * PAN + start : u * PAN + start + ROWS, q * 128 : (q + 1) * 128]
                y = y.reshape(ROWS // 8, 8, 128)
                for e in range(D):
                    term = y * mix_ref[column, (u * PAIRS + q) * D + e][None]
                    acc[e] = term if acc[e] is None else acc[e] + term
        for q in range(PAIRS):
            even, odd = acc[2 * q].reshape(ROWS, 128), acc[2 * q + 1].reshape(ROWS, 128)
            straight = jnp.where(low, even, odd)
            crossed = jnp.where(low, odd, even)
            both = straight + pltpu.roll(crossed, KB, 1)
            res_ref[start : start + ROWS, q * 128 : (q + 1) * 128] = both.astype(jnp.bfloat16)


def dot_and_mix(y_out, band_ref, rhs, y_in, mix_ref, column, res_ref):
    step, part = STACK // SPLIT, PAN // SPLIT
    for i in range(SPLIT):
        rows = slice(i * step, (i + 1) * step)
        y_out[rows, :] = jnp.dot(band_ref[0, rows, :], rhs, preferred_element_type=jnp.float32)
        mix_rows(y_in, mix_ref, column, res_ref, range(i * part, (i + 1) * part, ROWS))


def turn_kernel(
    panels, odd_first, count,
    flag_ref, left_in_ref, left_ref, left_out_ref, in_ref, mid_ref, out_ref, ca_ref, cb_ref, mix_ref,
    keep_ref, send_ref, pass_ref,
    src, ya, yb, wide, res_a, res_b,
):
    s = pl.program_id(0)
    is_odd_home = flag_ref[0]
    is_first = flag_ref[1]
    inner_at = jnp.where(flag_ref[3] == 0, panels + 2, 0)
    outer_at = panels + 2 - inner_at
    even_total = panels + 2
    dump = 2 * panels + 6

    @pl.when(s == 0)
    def _():
        @pl.when(is_first == 1)
        def _():
            src[pl.ds(inner_at, 2)] = left_in_ref[0]
            src[2 : panels + 2] = left_ref[0]
            src[pl.ds(outer_at, 2)] = left_out_ref[0]

        @pl.when(is_first == 0)
        def _():
            src[pl.ds(inner_at, 2)] = in_ref[...]
            src[2 : panels + 2] = mid_ref[...]
            src[pl.ds(outer_at, 2)] = out_ref[...]

        for column in range(2):
            for i in range(TERMS):
                wide[column, i] = jnp.broadcast_to(mix_ref[0, column, i : i + 1, :], (8, 128))

    def window(n):
        odd = jnp.clip(n - odd_first, 0, panels - 1) + panels + 4
        base = jnp.where(n < odd_first, jnp.minimum(n, panels + 1), odd)
        return src[pl.ds(base, 3)].reshape(BAND, LANES)

    def hand_out(n, res):
        slot = jnp.where((n >= 0) & (n < even_total), panels + 4 + n, dump)
        src[pl.ds(slot, 1)] = res[...][None]
        own_even = (n >= 1) & (n <= panels)
        own_odd = (n >= odd_first) & (n < odd_first + panels)
        to_keep = jnp.where(is_odd_home == 1, own_odd, own_even)
        to_send = jnp.where(is_odd_home == 1, own_even, own_odd)
        at_even = jnp.clip(n - 1, 0, panels - 1)
        at_odd = jnp.clip(n - odd_first, 0, panels - 1)
        at = jnp.where(own_odd, at_odd, at_even)

        @pl.when(to_keep)
        def _():
            keep_ref[pl.ds(at, 1)] = res[...][None]

        @pl.when(to_send)
        def _():
            send_ref[pl.ds(at, 1)] = res[...][None]

        @pl.when(own_odd)
        def _():
            pass_ref[pl.ds(at, 1)] = res[...][None]

    def phase(n):
        return (n >= odd_first).astype(jnp.int32)

    n = 2 * s

    @pl.when(s < count // 2)
    def _():
        dot_and_mix(ya, ca_ref, window(n), yb, wide, phase(n - 1), res_b)
        hand_out(n - 1, res_b)
        dot_and_mix(yb, cb_ref, window(n + 1), ya, wide, phase(n), res_a)
        hand_out(n, res_a)

    @pl.when(s == count // 2)
    def _():
        mix_rows(yb, wide, phase(n - 1), res_b, range(0, PAN, ROWS))
        hand_out(n - 1, res_b)


def one_turn(flags, left, inner, mid, outer, bands, mixing):
    panels = mid.shape[0]
    gap = 0 if panels >= 2 else 1
    odd_first = panels + 2 + gap
    count = odd_first + panels
    count += count % 2
    last = 2 * panels + 1

    def band_at(n):
        return jnp.minimum(jnp.where(n < odd_first, jnp.minimum(n, panels + 1), n - gap), last)

    block = jax.ShapeDtypeStruct((panels, PAN, LANES), jnp.bfloat16)
    whole = lambda shape: pl.BlockSpec(shape, lambda s, f: (0,) * len(shape))
    spec = pltpu.PrefetchScalarGridSpec(
        num_scalar_prefetch=1,
        grid=(count // 2 + 1,),
        in_specs=[
            pl.BlockSpec((1, 2, PAN, LANES), lambda s, f: (f[2], 0, 0, 0)),
            pl.BlockSpec((1, panels, PAN, LANES), lambda s, f: (f[2], 0, 0, 0)),
            pl.BlockSpec((1, 2, PAN, LANES), lambda s, f: (f[2], 0, 0, 0)),
            whole((2, PAN, LANES)),
            whole((panels, PAN, LANES)),
            whole((2, PAN, LANES)),
            pl.BlockSpec((1, STACK, BAND), lambda s, f: (band_at(2 * s), 0, 0)),
            pl.BlockSpec((1, STACK, BAND), lambda s, f: (band_at(2 * s + 1), 0, 0)),
            pl.BlockSpec((1, 2, TERMS, 128), lambda s, f: (f[2], 0, 0, 0)),
        ],
        out_specs=[whole((panels, PAN, LANES))] * 3,
        scratch_shapes=[
            pltpu.VMEM((2 * panels + 7, PAN, LANES), jnp.bfloat16),
            pltpu.VMEM((STACK, LANES), jnp.float32),
            pltpu.VMEM((STACK, LANES), jnp.float32),
            pltpu.VMEM((2, TERMS, 8, 128), jnp.float32),
            pltpu.VMEM((PAN, LANES), jnp.bfloat16),
            pltpu.VMEM((PAN, LANES), jnp.bfloat16),
        ],
    )
    steps = 2 * panels + 2
    return pl.pallas_call(
        functools.partial(turn_kernel, panels, odd_first, count),
        grid_spec=spec,
        out_shape=[block] * 3,
        compiler_params=pltpu.CompilerParams(vmem_limit_bytes=40 * MIB),
        cost_estimate=pl.CostEstimate(
            flops=steps * 2 * STACK * BAND * LANES * 2,
            bytes_accessed=steps * STACK * BAND * 2 * 3,
            transcendentals=0,
        ),
        name="two_columns",
    )(flags, *left, inner, mid, outer, bands, bands, mixing)


def pack_kernel(at_ref, left_ref, out_ref):
    low = lax.broadcasted_iota(jnp.int32, (PAN, 128), 1) < KB
    for q in range(PAIRS):
        even = left_ref[2 * q].astype(jnp.float32)
        odd = left_ref[2 * q + 1].astype(jnp.float32)
        first = jnp.where(low, even, pltpu.roll(odd, KB, 1))
        second = jnp.where(low, pltpu.roll(even, KB, 1), odd)
        out_ref[0, 0, :, q * 128 : (q + 1) * 128] = first.astype(jnp.bfloat16)
        out_ref[1, 0, :, q * 128 : (q + 1) * 128] = second.astype(jnp.bfloat16)


def packed(at, left, blocks):
    panels = left.shape[1] // PAN
    return pl.pallas_call(
        pack_kernel,
        grid_spec=pltpu.PrefetchScalarGridSpec(
            num_scalar_prefetch=1,
            grid=(blocks // 2, panels),
            in_specs=[pl.BlockSpec((D, PAN, 128), lambda c, p, f: (0, p, f[0] + c))],
            out_specs=pl.BlockSpec((2, 1, PAN, LANES), lambda c, p, f: (c, p, 0, 0)),
        ),
        out_shape=jax.ShapeDtypeStruct((blocks, panels, PAN, LANES), jnp.bfloat16),
        compiler_params=pltpu.CompilerParams(vmem_limit_bytes=32 * MIB),
        name="pack",
    )(at, left)


def unpack_kernel(at_ref, ka_ref, kb_ref, ga_ref, gb_ref, *rest):
    out_ref = rest[-1]
    low = lax.broadcasted_iota(jnp.int32, (PAN, 128), 1) < KB
    own = pl.program_id(0) == 0
    for q in range(PAIRS):
        lanes = slice(q * 128, (q + 1) * 128)
        one = jnp.where(own, ka_ref[0, :, lanes].astype(jnp.float32), ga_ref[0, :, lanes].astype(jnp.float32))
        two = jnp.where(own, kb_ref[0, :, lanes].astype(jnp.float32), gb_ref[0, :, lanes].astype(jnp.float32))
        first = jnp.where(low, one, pltpu.roll(two, KB, 1))
        second = jnp.where(low, pltpu.roll(one, KB, 1), two)
        out_ref[2 * q] = first.astype(jnp.bfloat16)
        out_ref[2 * q + 1] = second.astype(jnp.bfloat16)


def unpacked(at, held, shape, parts):
    panels = parts[0].shape[0]
    one = pl.BlockSpec((1, PAN, LANES), lambda s, p, f: (p, 0, 0))
    more = [] if held is None else [held]
    return pl.pallas_call(
        unpack_kernel,
        grid_spec=pltpu.PrefetchScalarGridSpec(
            num_scalar_prefetch=1,
            grid=(2, panels),
            in_specs=[one] * 4 + [pl.BlockSpec(memory_space=pl.ANY)] * len(more),
            out_specs=pl.BlockSpec((D, PAN, 128), lambda s, p, f: (0, p, f[s])),
        ),
        out_shape=jax.ShapeDtypeStruct(shape, jnp.bfloat16),
        input_output_aliases={5: 0} if more else {},
        compiler_params=pltpu.CompilerParams(vmem_limit_bytes=32 * MIB),
        name="unpack",
    )(at, *parts, *more)


def far_edges(block, width, dim):
    count = lax.axis_size("sec")
    have = block.shape[dim]
    low_parts, high_parts = [], []
    reach = 0
    while width > reach:
        hop = reach // have + 1
        take = min(have, width - reach)
        forward = [(i, i + hop) for i in range(count - hop)]
        backward = [(i + hop, i) for i in range(count - hop)]
        top = lax.slice_in_dim(block, have - take, have, axis=dim)
        bottom = lax.slice_in_dim(block, 0, take, axis=dim)
        low_parts.insert(0, lax.ppermute(top, "sec", forward))
        high_parts.append(lax.ppermute(bottom, "sec", backward))
        reach += take
    low, high = jnp.concatenate(low_parts, dim), jnp.concatenate(high_parts, dim)
    first = lax.axis_index("sec") % 2 == 0
    return jnp.where(first, high, low), jnp.where(first, low, high)


def side(block, width, dim, towards_inner):
    first = lax.axis_index("sec") % 2 == 0
    top_wanted = first if towards_inner else jnp.logical_not(first)
    start = jnp.where(top_wanted, block.shape[dim] - width, 0)
    return lax.dynamic_slice_in_dim(block, start, width, dim)


def inner_edge(block, width, dim=0):
    pairs = [(i, i ^ 1) for i in range(lax.axis_size("sec"))]
    return lax.ppermute(side(block, width, dim, True), "sec", pairs)


def outer_pairs():
    count = lax.axis_size("sec")
    forward = [(i, i + 1) for i in range(1, count - 1, 2)]
    return forward + [(j, i) for i, j in forward]


def both_edges(block, width, dim=0):
    if block.shape[dim] < width:
        return far_edges(block, width, dim)
    outer = lax.ppermute(side(block, width, dim, False), "sec", outer_pairs())
    return inner_edge(block, width, dim), outer


def on_device(left_start, coupling, tensor, sketch, block_parity, leg_parity):
    row_count, _, rank = left_start.shape
    panels = row_count // PAN
    col_count = lax.axis_size("col")
    sec_count = lax.axis_size("sec")
    col_index = lax.axis_index("col")
    sec_index = lax.axis_index("sec")
    stage = col_index // 2
    half = col_index % 2
    stages = col_count // 2
    half_cols = rank // 2
    blocks = half_cols // KB
    swap = [(i, i ^ 1) for i in range(col_count)]
    up = [(i, i + 2) for i in range(col_count - 2)]

    legs = lax.dynamic_index_in_dim(leg_parity, col_index, 0, keepdims=False)
    parity = lax.dynamic_slice_in_dim(
        jnp.pad(block_parity, (1, 1)), sec_index * panels, panels + 2, 0
    )
    table = 1.0 - 2.0 * (parity[:, None] * legs[None, :]).astype(jnp.float32)
    signs = jnp.stack([table[w : w + panels] for w in range(3)], 1).reshape(panels, 3 * D)
    own = ordered_coupling(coupling[0], signs)
    odd_home = half == 1
    rim = jnp.concatenate([own[:1], own[panels - 1 :]], 0) if panels > 1 else own
    other_rim = lax.ppermute(rim, "col", swap)
    own_inner, own_outer = both_edges(rim, 1)

    small = jnp.concatenate([tensor[0].reshape(D, D * D * D), sketch[0]], 1)
    small_other = lax.ppermute(small, "col", swap)

    def mixing_of(both):
        legs_part = both[:, : D * D * D].reshape(D, D, D, D)
        cols = lax.dynamic_slice_in_dim(both, D * D * D + half * half_cols, half_cols, 1)
        m = jnp.einsum("duez,zk->duek", legs_part, cols, precision=lax.Precision.HIGHEST)
        m = m.reshape(PAIRS, 2, D, D, blocks, KB).transpose(4, 2, 0, 3, 1, 5)
        return m.reshape(blocks, TERMS, 2 * KB)

    mixing = jnp.stack(
        [
            mixing_of(jnp.where(odd_home, small_other, small)),
            mixing_of(jnp.where(odd_home, small, small_other)),
        ],
        1,
    )

    at_half = (half * (blocks // 2)).astype(jnp.int32)[None]
    mine = packed(at_half, left_start.transpose(1, 0, 2), blocks)
    left_inner, left_outer = both_edges(mine, 2, 1)

    if panels > 2:
        inner = own[1 : panels - 1]
        other_inner = lax.ppermute(inner, "col", swap)
        other = [other_rim[:1], other_inner, other_rim[1:]]
        mine_too = [own[:1], own[1 : panels - 1], own[panels - 1 :]]
    else:
        other, mine_too = [other_rim], [own]
    other_inner_edge, other_outer_edge = both_edges(other_rim, 1)
    even_inner = jnp.where(odd_home, other_inner_edge, own_inner)
    even_outer = jnp.where(odd_home, other_outer_edge, own_outer)
    first_core = sec_index % 2 == 0
    even_low = jnp.where(first_core, even_outer, even_inner)
    even_high = jnp.where(first_core, even_inner, even_outer)
    even_bands = [
        jnp.where(odd_home, b, a)
        for a, b in zip(mine_too, other)
    ]
    odd_bands = [jnp.where(odd_home, a, b) for a, b in zip(mine_too, other)]
    even_bands = [even_low] + even_bands + [even_high]
    left_inner, left_outer, mixing, *rest = lax.optimization_barrier(
        (left_inner, left_outer, mixing, *even_bands, *odd_bands)
    )
    bands = jnp.concatenate(rest, 0)
    left = (left_inner, mine, left_outer)

    skew = SKEW
    turns = blocks + skew * (stages - 1)
    zero_edge = jnp.zeros((2, PAN, LANES), jnp.bfloat16)
    zero_mid = jnp.zeros((panels, PAN, LANES), jnp.bfloat16)
    arrived = {t: (zero_edge, zero_mid, zero_edge) for t in range(skew)}
    keeps, sends = {}, {}
    kept = []
    lag = skew * (stages - 1)

    def staged(table_of, i):
        out = table_of[i + lag]
        for z in range(stages - 1):
            out = jnp.where(stage == z, table_of[i + skew * z], out)
        return out

    flying, swapping = {}, {}
    states = None
    across = [
        (c * sec_count + i, (c + 2) * sec_count + j)
        for c in range(col_count - 2)
        for i, j in outer_pairs()
    ]
    direct = panels >= 2
    for t in range(turns):
        index = jnp.clip(t - skew * stage, 0, blocks - 1)
        flags = jnp.stack([half, (stage == 0).astype(jnp.int32), index, sec_index % 2])
        flags = flags.astype(jnp.int32)
        inner, mid, outer = arrived.pop(t)
        if t - 2 in swapping:
            flags, swapping[t - 2] = lax.optimization_barrier((flags, swapping[t - 2]))
        keeps[t], sends[t], passed = one_turn(flags, left, inner, mid, outer, bands, mixing)
        if t - 1 in flying:
            (nxt, outer), passed = lax.optimization_barrier((flying[t - 1], passed))
            if direct:
                inner = inner_edge(nxt, 2)
            else:
                inner, outer = far_edges(nxt, 2, 0)
            arrived[t - 1 + skew] = (inner, nxt, outer)
        if t + skew < turns:
            nxt = lax.ppermute(passed, "col", up)
            edge = nxt
            if direct:
                edge = lax.ppermute(side(passed, 2, 0, False), ("col", "sec"), across)
            flying[t] = (nxt, edge)
        if t >= lag:
            i = t - lag
            swapping[t] = lax.ppermute(staged(sends, i), "col", swap)
            kept.append(staged(keeps, i))
        for j in range(1, blocks, 2):
            if t == j + lag + 2 or (t == turns - 1 and j + lag + 2 > t):
                at = jnp.stack([half, 1 - half]) * (blocks // 2) + j // 2
                parts = (kept[j - 1], kept[j], swapping[j - 1 + lag], swapping[j + lag])
                states = unpacked(at.astype(jnp.int32), states, (D, row_count, rank), parts)

    flat = states.reshape(D * row_count, rank)
    share = rank // sec_count
    group = sec_count // 2
    top = sec_index // group
    halves = {}
    for name, which in (("far", 1 - top), ("near", top)):
        columns = lax.dynamic_slice_in_dim(flat, which * (rank // 2), rank // 2, 1)
        if name == "near":
            columns, far_now = lax.optimization_barrier((columns, halves["far"]))
            halves["far"] = far_now
            crossed = lax.ppermute(far_now, "sec", [(i, i ^ group) for i in range(sec_count)])
        gram = lax.dot_general(
            columns, flat, (((0,), (0,)), ((), ())), preferred_element_type=jnp.float32
        ).astype(jnp.bfloat16)
        gram = gram.reshape(group, share, rank)
        width = 1
        while width < group:
            bit = (sec_index // width) % 2
            pairs = gram.reshape(-1, 2, share, rank)
            stay = lax.dynamic_index_in_dim(pairs, bit, 1, keepdims=False)
            away = lax.dynamic_index_in_dim(pairs, 1 - bit, 1, keepdims=False)
            come = lax.ppermute(away, "sec", [(i, i ^ width) for i in range(sec_count)])
            gram = stay.astype(jnp.float32) + come.astype(jnp.float32)
            if name == "far" or gram.shape[0] > 1:
                gram = gram.astype(jnp.bfloat16)
            width *= 2
        halves[name] = gram
    gram_out = (halves["near"].astype(jnp.float32) + crossed.astype(jnp.float32)) * (1.0 / (CHI * D))
    return states.transpose(1, 0, 2)[None], gram_out


def solution(mesh):
    in_specs = (
        P("sec", None, None),
        P("col", "sec", None),
        P("col", None, None, None, None),
        P("col", None, None),
        P(),
        P(),
    )
    out_specs = (P("col", "sec", None, None), P("col", "sec", None))
    return jax.shard_map(
        on_device, mesh=mesh, in_specs=in_specs, out_specs=out_specs, check_vma=False
    )
```

```python
import functools

import jax
import jax.numpy as jnp
from jax import lax
from jax.experimental import pallas as pl
from jax.experimental.pallas import tpu as pltpu
from jax.sharding import PartitionSpec as P

CHI = 2048
D = 6
PAN = 128
KB = 64
PAIRS = D // 2
LANES = PAIRS * 2 * KB
STACK = D * PAN
BAND = 3 * PAN
TERMS = D * PAIRS * D
ROWS = 32
SPLIT = 2
SKEW = 2
TURN_VMEM = 50
MIB = 1024 * 1024


def ordering_matrix():
    row = lax.broadcasted_iota(jnp.int32, (STACK, STACK), 0)
    col = lax.broadcasted_iota(jnp.int32, (STACK, STACK), 1)
    return (col == (row % D) * PAN + row // D).astype(jnp.bfloat16)


def order_kernel(sign_ref, band_ref, perm_ref, out_ref):
    p, w = pl.program_id(0), pl.program_id(1)
    moved = jnp.dot(band_ref[...], perm_ref[...], preferred_element_type=jnp.float32)
    for u in range(D):
        part = moved[:, u * PAN : (u + 1) * PAN] * sign_ref[p, w * D + u]
        out_ref[0, u * PAN : (u + 1) * PAN, :] = part.astype(jnp.bfloat16)


def ordered_coupling(coupling, signs):
    rows = coupling.shape[0]
    panels = rows // PAN
    return pl.pallas_call(
        order_kernel,
        grid=(panels, 3),
        in_specs=[
            pl.BlockSpec(memory_space=pltpu.SMEM),
            pl.BlockSpec((PAN, STACK), lambda p, w: (p, w)),
            pl.BlockSpec((STACK, STACK), lambda p, w: (0, 0)),
        ],
        out_specs=pl.BlockSpec((1, STACK, PAN), lambda p, w: (p, 0, w)),
        out_shape=jax.ShapeDtypeStruct((panels, STACK, BAND), jnp.bfloat16),
        compiler_params=pltpu.CompilerParams(vmem_limit_bytes=32 * MIB),
        name="order_coupling",
    )(signs, coupling, ordering_matrix())


def mix_rows(y_ref, mix_ref, column, res_ref, starts):
    low = lax.broadcasted_iota(jnp.int32, (ROWS, 2 * KB), 1) < KB
    for start in starts:
        acc = [None] * D
        for u in range(D):
            for q in range(PAIRS):
                y = y_ref[u * PAN + start : u * PAN + start + ROWS, q * 128 : (q + 1) * 128]
                y = y.reshape(ROWS // 8, 8, 128)
                for e in range(D):
                    term = y * mix_ref[column, (u * PAIRS + q) * D + e][None]
                    acc[e] = term if acc[e] is None else acc[e] + term
        for q in range(PAIRS):
            even, odd = acc[2 * q].reshape(ROWS, 128), acc[2 * q + 1].reshape(ROWS, 128)
            straight = jnp.where(low, even, odd)
            crossed = jnp.where(low, odd, even)
            both = straight + pltpu.roll(crossed, KB, 1)
            res_ref[start : start + ROWS, q * 128 : (q + 1) * 128] = both.astype(jnp.bfloat16)


def dot_and_mix(y_out, band_ref, rhs, y_in, mix_ref, column, res_ref):
    step, part = STACK // SPLIT, PAN // SPLIT
    for i in range(SPLIT):
        rows = slice(i * step, (i + 1) * step)
        y_out[rows, :] = jnp.dot(band_ref[0, rows, :], rhs, preferred_element_type=jnp.float32)
        mix_rows(y_in, mix_ref, column, res_ref, range(i * part, (i + 1) * part, ROWS))


def turn_kernel(
    panels, odd_first, count,
    flag_ref, left_in_ref, left_ref, left_out_ref, in_ref, mid_ref, out_ref, ca_ref, cb_ref, mix_ref,
    keep_ref, send_ref, pass_ref,
    src, ya, yb, wide, res_a, res_b,
):
    s = pl.program_id(0)
    is_odd_home = flag_ref[0]
    is_first = flag_ref[1]
    inner_at = jnp.where(flag_ref[3] == 0, panels + 2, 0)
    outer_at = panels + 2 - inner_at
    even_total = panels + 2
    dump = 2 * panels + 6

    @pl.when(s == 0)
    def _():
        @pl.when(is_first == 1)
        def _():
            src[pl.ds(inner_at, 2)] = left_in_ref[0]
            src[2 : panels + 2] = left_ref[0]
            src[pl.ds(outer_at, 2)] = left_out_ref[0]

        @pl.when(is_first == 0)
        def _():
            src[pl.ds(inner_at, 2)] = in_ref[...]
            src[2 : panels + 2] = mid_ref[...]
            src[pl.ds(outer_at, 2)] = out_ref[...]

        for column in range(2):
            for i in range(TERMS):
                wide[column, i] = jnp.broadcast_to(mix_ref[0, column, i : i + 1, :], (8, 128))

    def window(n):
        odd = jnp.clip(n - odd_first, 0, panels - 1) + panels + 4
        base = jnp.where(n < odd_first, jnp.minimum(n, panels + 1), odd)
        return src[pl.ds(base, 3)].reshape(BAND, LANES)

    def hand_out(n, res):
        slot = jnp.where((n >= 0) & (n < even_total), panels + 4 + n, dump)
        src[pl.ds(slot, 1)] = res[...][None]
        own_even = (n >= 1) & (n <= panels)
        own_odd = (n >= odd_first) & (n < odd_first + panels)
        to_keep = jnp.where(is_odd_home == 1, own_odd, own_even)
        to_send = jnp.where(is_odd_home == 1, own_even, own_odd)
        at_even = jnp.clip(n - 1, 0, panels - 1)
        at_odd = jnp.clip(n - odd_first, 0, panels - 1)
        at = jnp.where(own_odd, at_odd, at_even)

        @pl.when(to_keep)
        def _():
            keep_ref[pl.ds(at, 1)] = res[...][None]

        @pl.when(to_send)
        def _():
            send_ref[pl.ds(at, 1)] = res[...][None]

        @pl.when(own_odd)
        def _():
            pass_ref[pl.ds(at, 1)] = res[...][None]

    def phase(n):
        return (n >= odd_first).astype(jnp.int32)

    n = 2 * s

    @pl.when(s < count // 2)
    def _():
        dot_and_mix(ya, ca_ref, window(n), yb, wide, phase(n - 1), res_b)
        hand_out(n - 1, res_b)
        dot_and_mix(yb, cb_ref, window(n + 1), ya, wide, phase(n), res_a)
        hand_out(n, res_a)

    @pl.when(s == count // 2)
    def _():
        mix_rows(yb, wide, phase(n - 1), res_b, range(0, PAN, ROWS))
        hand_out(n - 1, res_b)


def one_turn(flags, left, inner, mid, outer, bands, mixing):
    panels = mid.shape[0]
    gap = 0 if panels >= 2 else 1
    odd_first = panels + 2 + gap
    count = odd_first + panels
    count += count % 2
    last = 2 * panels + 1

    def band_at(n):
        return jnp.minimum(jnp.where(n < odd_first, jnp.minimum(n, panels + 1), n - gap), last)

    block = jax.ShapeDtypeStruct((panels, PAN, LANES), jnp.bfloat16)
    whole = lambda shape: pl.BlockSpec(shape, lambda s, f: (0,) * len(shape))
    spec = pltpu.PrefetchScalarGridSpec(
        num_scalar_prefetch=1,
        grid=(count // 2 + 1,),
        in_specs=[
            pl.BlockSpec((1, 2, PAN, LANES), lambda s, f: (f[2], 0, 0, 0)),
            pl.BlockSpec((1, panels, PAN, LANES), lambda s, f: (f[2], 0, 0, 0)),
            pl.BlockSpec((1, 2, PAN, LANES), lambda s, f: (f[2], 0, 0, 0)),
            whole((2, PAN, LANES)),
            whole((panels, PAN, LANES)),
            whole((2, PAN, LANES)),
            pl.BlockSpec((1, STACK, BAND), lambda s, f: (band_at(2 * s), 0, 0)),
            pl.BlockSpec((1, STACK, BAND), lambda s, f: (band_at(2 * s + 1), 0, 0)),
            pl.BlockSpec((1, 2, TERMS, 128), lambda s, f: (f[2], 0, 0, 0)),
        ],
        out_specs=[whole((panels, PAN, LANES))] * 3,
        scratch_shapes=[
            pltpu.VMEM((2 * panels + 7, PAN, LANES), jnp.bfloat16),
            pltpu.VMEM((STACK, LANES), jnp.float32),
            pltpu.VMEM((STACK, LANES), jnp.float32),
            pltpu.VMEM((2, TERMS, 8, 128), jnp.float32),
            pltpu.VMEM((PAN, LANES), jnp.bfloat16),
            pltpu.VMEM((PAN, LANES), jnp.bfloat16),
        ],
    )
    steps = 2 * panels + 2
    return pl.pallas_call(
        functools.partial(turn_kernel, panels, odd_first, count),
        grid_spec=spec,
        out_shape=[block] * 3,
        compiler_params=pltpu.CompilerParams(vmem_limit_bytes=TURN_VMEM * MIB),
        cost_estimate=pl.CostEstimate(
            flops=steps * 2 * STACK * BAND * LANES * 2,
            bytes_accessed=steps * STACK * BAND * 2 * 3,
            transcendentals=0,
        ),
        name="two_columns",
    )(flags, *left, inner, mid, outer, bands, bands, mixing)


def pack_kernel(at_ref, left_ref, out_ref):
    low = lax.broadcasted_iota(jnp.int32, (PAN, 128), 1) < KB
    for q in range(PAIRS):
        even = left_ref[2 * q].astype(jnp.float32)
        odd = left_ref[2 * q + 1].astype(jnp.float32)
        first = jnp.where(low, even, pltpu.roll(odd, KB, 1))
        second = jnp.where(low, pltpu.roll(even, KB, 1), odd)
        out_ref[0, 0, :, q * 128 : (q + 1) * 128] = first.astype(jnp.bfloat16)
        out_ref[1, 0, :, q * 128 : (q + 1) * 128] = second.astype(jnp.bfloat16)


def packed(at, left, blocks):
    panels = left.shape[1] // PAN
    return pl.pallas_call(
        pack_kernel,
        grid_spec=pltpu.PrefetchScalarGridSpec(
            num_scalar_prefetch=1,
            grid=(blocks // 2, panels),
            in_specs=[pl.BlockSpec((D, PAN, 128), lambda c, p, f: (0, p, f[0] + c))],
            out_specs=pl.BlockSpec((2, 1, PAN, LANES), lambda c, p, f: (c, p, 0, 0)),
        ),
        out_shape=jax.ShapeDtypeStruct((blocks, panels, PAN, LANES), jnp.bfloat16),
        compiler_params=pltpu.CompilerParams(vmem_limit_bytes=32 * MIB),
        name="pack",
    )(at, left)


def unpack_kernel(at_ref, ka_ref, kb_ref, ga_ref, gb_ref, *rest):
    out_ref = rest[-1]
    low = lax.broadcasted_iota(jnp.int32, (PAN, 128), 1) < KB
    own = pl.program_id(0) == 0
    for q in range(PAIRS):
        lanes = slice(q * 128, (q + 1) * 128)
        one = jnp.where(own, ka_ref[0, :, lanes].astype(jnp.float32), ga_ref[0, :, lanes].astype(jnp.float32))
        two = jnp.where(own, kb_ref[0, :, lanes].astype(jnp.float32), gb_ref[0, :, lanes].astype(jnp.float32))
        first = jnp.where(low, one, pltpu.roll(two, KB, 1))
        second = jnp.where(low, pltpu.roll(one, KB, 1), two)
        out_ref[2 * q] = first.astype(jnp.bfloat16)
        out_ref[2 * q + 1] = second.astype(jnp.bfloat16)


def unpacked(at, held, shape, parts):
    panels = parts[0].shape[0]
    one = pl.BlockSpec((1, PAN, LANES), lambda s, p, f: (p, 0, 0))
    more = [] if held is None else [held]
    return pl.pallas_call(
        unpack_kernel,
        grid_spec=pltpu.PrefetchScalarGridSpec(
            num_scalar_prefetch=1,
            grid=(2, panels),
            in_specs=[one] * 4 + [pl.BlockSpec(memory_space=pl.ANY)] * len(more),
            out_specs=pl.BlockSpec((D, PAN, 128), lambda s, p, f: (0, p, f[s])),
        ),
        out_shape=jax.ShapeDtypeStruct(shape, jnp.bfloat16),
        input_output_aliases={5: 0} if more else {},
        compiler_params=pltpu.CompilerParams(vmem_limit_bytes=32 * MIB),
        name="unpack",
    )(at, *parts, *more)


def far_edges(block, width, dim):
    count = lax.axis_size("sec")
    have = block.shape[dim]
    low_parts, high_parts = [], []
    reach = 0
    while width > reach:
        hop = reach // have + 1
        take = min(have, width - reach)
        forward = [(i, i + hop) for i in range(count - hop)]
        backward = [(i + hop, i) for i in range(count - hop)]
        top = lax.slice_in_dim(block, have - take, have, axis=dim)
        bottom = lax.slice_in_dim(block, 0, take, axis=dim)
        low_parts.insert(0, lax.ppermute(top, "sec", forward))
        high_parts.append(lax.ppermute(bottom, "sec", backward))
        reach += take
    low, high = jnp.concatenate(low_parts, dim), jnp.concatenate(high_parts, dim)
    first = lax.axis_index("sec") % 2 == 0
    return jnp.where(first, high, low), jnp.where(first, low, high)


def side(block, width, dim, towards_inner):
    first = lax.axis_index("sec") % 2 == 0
    top_wanted = first if towards_inner else jnp.logical_not(first)
    start = jnp.where(top_wanted, block.shape[dim] - width, 0)
    return lax.dynamic_slice_in_dim(block, start, width, dim)


def inner_edge(block, width, dim=0):
    pairs = [(i, i ^ 1) for i in range(lax.axis_size("sec"))]
    return lax.ppermute(side(block, width, dim, True), "sec", pairs)


def outer_pairs():
    count = lax.axis_size("sec")
    forward = [(i, i + 1) for i in range(1, count - 1, 2)]
    return forward + [(j, i) for i, j in forward]


def both_edges(block, width, dim=0):
    if block.shape[dim] < width:
        return far_edges(block, width, dim)
    outer = lax.ppermute(side(block, width, dim, False), "sec", outer_pairs())
    return inner_edge(block, width, dim), outer


def on_device(left_start, coupling, tensor, sketch, block_parity, leg_parity):
    row_count, _, rank = left_start.shape
    panels = row_count // PAN
    col_count = lax.axis_size("col")
    sec_count = lax.axis_size("sec")
    col_index = lax.axis_index("col")
    sec_index = lax.axis_index("sec")
    stage = col_index // 2
    half = col_index % 2
    stages = col_count // 2
    half_cols = rank // 2
    blocks = half_cols // KB
    swap = [(i, i ^ 1) for i in range(col_count)]
    up = [(i, i + 2) for i in range(col_count - 2)]

    legs = lax.dynamic_index_in_dim(leg_parity, col_index, 0, keepdims=False)
    parity = lax.dynamic_slice_in_dim(
        jnp.pad(block_parity, (1, 1)), sec_index * panels, panels + 2, 0
    )
    table = 1.0 - 2.0 * (parity[:, None] * legs[None, :]).astype(jnp.float32)
    signs = jnp.stack([table[w : w + panels] for w in range(3)], 1).reshape(panels, 3 * D)
    own = ordered_coupling(coupling[0], signs)
    odd_home = half == 1
    rim = jnp.concatenate([own[:1], own[panels - 1 :]], 0) if panels > 1 else own
    other_rim = lax.ppermute(rim, "col", swap)
    own_inner, own_outer = both_edges(rim, 1)

    small = jnp.concatenate([tensor[0].reshape(D, D * D * D), sketch[0]], 1)
    small_other = lax.ppermute(small, "col", swap)

    def mixing_of(both):
        legs_part = both[:, : D * D * D].reshape(D, D, D, D)
        cols = lax.dynamic_slice_in_dim(both, D * D * D + half * half_cols, half_cols, 1)
        m = jnp.einsum("duez,zk->duek", legs_part, cols, precision=lax.Precision.HIGHEST)
        m = m.reshape(PAIRS, 2, D, D, blocks, KB).transpose(4, 2, 0, 3, 1, 5)
        return m.reshape(blocks, TERMS, 2 * KB)

    mixing = jnp.stack(
        [
            mixing_of(jnp.where(odd_home, small_other, small)),
            mixing_of(jnp.where(odd_home, small, small_other)),
        ],
        1,
    )

    at_half = (half * (blocks // 2)).astype(jnp.int32)[None]
    mine = packed(at_half, left_start.transpose(1, 0, 2), blocks)
    left_inner, left_outer = both_edges(mine, 2, 1)

    if panels > 2:
        inner = own[1 : panels - 1]
        other_inner = lax.ppermute(inner, "col", swap)
        other = [other_rim[:1], other_inner, other_rim[1:]]
        mine_too = [own[:1], own[1 : panels - 1], own[panels - 1 :]]
    else:
        other, mine_too = [other_rim], [own]
    other_rim, mixing, mine = lax.optimization_barrier((other_rim, mixing, mine))
    other_inner_edge, other_outer_edge = both_edges(other_rim, 1)
    even_inner = jnp.where(odd_home, other_inner_edge, own_inner)
    even_outer = jnp.where(odd_home, other_outer_edge, own_outer)
    first_core = sec_index % 2 == 0
    even_low = jnp.where(first_core, even_outer, even_inner)
    even_high = jnp.where(first_core, even_inner, even_outer)
    even_bands = [
        jnp.where(odd_home, b, a)
        for a, b in zip(mine_too, other)
    ]
    odd_bands = [jnp.where(odd_home, a, b) for a, b in zip(mine_too, other)]
    even_bands = [even_low] + even_bands + [even_high]
    left_inner, left_outer, mixing, *rest = lax.optimization_barrier(
        (left_inner, left_outer, mixing, *even_bands, *odd_bands)
    )
    bands = jnp.concatenate(rest, 0)
    left = (left_inner, mine, left_outer)

    skew = SKEW
    turns = blocks + skew * (stages - 1)
    zero_edge = jnp.zeros((2, PAN, LANES), jnp.bfloat16)
    zero_mid = jnp.zeros((panels, PAN, LANES), jnp.bfloat16)
    arrived = {t: (zero_edge, zero_mid, zero_edge) for t in range(skew)}
    keeps, sends = {}, {}
    kept = []
    lag = skew * (stages - 1)

    def staged(table_of, i):
        out = table_of[i + lag]
        for z in range(stages - 1):
            out = jnp.where(stage == z, table_of[i + skew * z], out)
        return out

    flying, swapping = {}, {}
    states = None
    across = [
        (c * sec_count + i, (c + 2) * sec_count + j)
        for c in range(col_count - 2)
        for i, j in outer_pairs()
    ]
    direct = panels >= 2
    for t in range(turns):
        index = jnp.clip(t - skew * stage, 0, blocks - 1)
        flags = jnp.stack([half, (stage == 0).astype(jnp.int32), index, sec_index % 2])
        flags = flags.astype(jnp.int32)
        inner, mid, outer = arrived.pop(t)
        if t - 2 in swapping:
            flags, swapping[t - 2] = lax.optimization_barrier((flags, swapping[t - 2]))
        keeps[t], sends[t], passed = one_turn(flags, left, inner, mid, outer, bands, mixing)
        if t - 1 in flying:
            (nxt, outer), passed = lax.optimization_barrier((flying[t - 1], passed))
            if direct:
                inner = inner_edge(nxt, 2)
            else:
                inner, outer = far_edges(nxt, 2, 0)
            arrived[t - 1 + skew] = (inner, nxt, outer)
        if t + skew < turns:
            nxt = lax.ppermute(passed, "col", up)
            edge = nxt
            if direct:
                edge = lax.ppermute(side(passed, 2, 0, False), ("col", "sec"), across)
            flying[t] = (nxt, edge)
        if t >= lag:
            i = t - lag
            swapping[t] = lax.ppermute(staged(sends, i), "col", swap)
            kept.append(staged(keeps, i))
        for j in range(1, blocks, 2):
            if t == j + lag + 2 or (t == turns - 1 and j + lag + 2 > t):
                at = jnp.stack([half, 1 - half]) * (blocks // 2) + j // 2
                parts = (kept[j - 1], kept[j], swapping[j - 1 + lag], swapping[j + lag])
                states = unpacked(at.astype(jnp.int32), states, (D, row_count, rank), parts)

    flat = states.reshape(D * row_count, rank)
    share = rank // sec_count
    group = sec_count // 2
    top = sec_index // group
    halves = {}
    for name, which in (("far", 1 - top), ("near", top)):
        columns = lax.dynamic_slice_in_dim(flat, which * (rank // 2), rank // 2, 1)
        if name == "near":
            columns, far_now = lax.optimization_barrier((columns, halves["far"]))
            halves["far"] = far_now
            crossed = lax.ppermute(far_now, "sec", [(i, i ^ group) for i in range(sec_count)])
        gram = lax.dot_general(
            columns, flat, (((0,), (0,)), ((), ())), preferred_element_type=jnp.float32
        ).astype(jnp.bfloat16)
        gram = gram.reshape(group, share, rank)
        width = 1
        while width < group:
            bit = (sec_index // width) % 2
            pairs = gram.reshape(-1, 2, share, rank)
            stay = lax.dynamic_index_in_dim(pairs, bit, 1, keepdims=False)
            away = lax.dynamic_index_in_dim(pairs, 1 - bit, 1, keepdims=False)
            come = lax.ppermute(away, "sec", [(i, i ^ width) for i in range(sec_count)])
            gram = stay.astype(jnp.float32) + come.astype(jnp.float32)
            if name == "far" or gram.shape[0] > 1:
                gram = gram.astype(jnp.bfloat16)
            width *= 2
        halves[name] = gram
    gram_out = (halves["near"].astype(jnp.float32) + crossed.astype(jnp.float32)) * (1.0 / (CHI * D))
    return states.transpose(1, 0, 2)[None], gram_out


def solution(mesh):
    in_specs = (
        P("sec", None, None),
        P("col", "sec", None),
        P("col", None, None, None, None),
        P("col", None, None),
        P(),
        P(),
    )
    out_specs = (P("col", "sec", None, None), P("col", "sec", None))
    return jax.shard_map(
        on_device, mesh=mesh, in_specs=in_specs, out_specs=out_specs, check_vma=False
    )
```

```python
import functools

import jax
import jax.numpy as jnp
from jax import lax
from jax.experimental import pallas as pl
from jax.experimental.pallas import tpu as pltpu
from jax.sharding import PartitionSpec as P

CHI = 2048
D = 6
PAN = 128
KB = 64
PAIRS = D // 2
LANES = PAIRS * 2 * KB
STACK = D * PAN
BAND = 3 * PAN
TERMS = D * PAIRS * D
ROWS = 32
SPLIT = 2
SKEW = 2
TURN_VMEM = 50
MIB = 1024 * 1024


def ordering_matrix():
    row = lax.broadcasted_iota(jnp.int32, (STACK, STACK), 0)
    col = lax.broadcasted_iota(jnp.int32, (STACK, STACK), 1)
    return (col == (row % D) * PAN + row // D).astype(jnp.bfloat16)


def order_kernel(sign_ref, band_ref, perm_ref, out_ref):
    p, w = pl.program_id(0), pl.program_id(1)
    moved = jnp.dot(band_ref[...], perm_ref[...], preferred_element_type=jnp.float32)
    for u in range(D):
        part = moved[:, u * PAN : (u + 1) * PAN] * sign_ref[p, w * D + u]
        out_ref[0, u * PAN : (u + 1) * PAN, :] = part.astype(jnp.bfloat16)


def ordered_coupling(coupling, signs):
    rows = coupling.shape[0]
    panels = rows // PAN
    return pl.pallas_call(
        order_kernel,
        grid=(panels, 3),
        in_specs=[
            pl.BlockSpec(memory_space=pltpu.SMEM),
            pl.BlockSpec((PAN, STACK), lambda p, w: (p, w)),
            pl.BlockSpec((STACK, STACK), lambda p, w: (0, 0)),
        ],
        out_specs=pl.BlockSpec((1, STACK, PAN), lambda p, w: (p, 0, w)),
        out_shape=jax.ShapeDtypeStruct((panels, STACK, BAND), jnp.bfloat16),
        compiler_params=pltpu.CompilerParams(vmem_limit_bytes=32 * MIB),
        name="order_coupling",
    )(signs, coupling, ordering_matrix())


def mix_rows(y_ref, mix_ref, column, res_ref, starts):
    low = lax.broadcasted_iota(jnp.int32, (ROWS, 2 * KB), 1) < KB
    for start in starts:
        acc = [None] * D
        for u in range(D):
            for q in range(PAIRS):
                y = y_ref[u * PAN + start : u * PAN + start + ROWS, q * 128 : (q + 1) * 128]
                y = y.reshape(ROWS // 8, 8, 128)
                for e in range(D):
                    term = y * mix_ref[column, (u * PAIRS + q) * D + e][None]
                    acc[e] = term if acc[e] is None else acc[e] + term
        for q in range(PAIRS):
            even, odd = acc[2 * q].reshape(ROWS, 128), acc[2 * q + 1].reshape(ROWS, 128)
            straight = jnp.where(low, even, odd)
            crossed = jnp.where(low, odd, even)
            both = straight + pltpu.roll(crossed, KB, 1)
            res_ref[start : start + ROWS, q * 128 : (q + 1) * 128] = both.astype(jnp.bfloat16)


def dot_and_mix(y_out, band_ref, rhs, y_in, mix_ref, column, res_ref):
    step, part = STACK // SPLIT, PAN // SPLIT
    for i in range(SPLIT):
        rows = slice(i * step, (i + 1) * step)
        y_out[rows, :] = jnp.dot(band_ref[0, rows, :], rhs, preferred_element_type=jnp.float32)
        mix_rows(y_in, mix_ref, column, res_ref, range(i * part, (i + 1) * part, ROWS))


def turn_kernel(
    panels, odd_first, count,
    flag_ref, left_in_ref, left_ref, left_out_ref, in_ref, mid_ref, out_ref, ca_ref, cb_ref, mix_ref,
    keep_ref, send_ref, pass_ref,
    src, ya, yb, wide, res_a, res_b,
):
    s = pl.program_id(0)
    is_odd_home = flag_ref[0]
    is_first = flag_ref[1]
    inner_at = jnp.where(flag_ref[3] == 0, panels + 2, 0)
    outer_at = panels + 2 - inner_at
    even_total = panels + 2
    dump = 2 * panels + 6

    @pl.when(s == 0)
    def _():
        @pl.when(is_first == 1)
        def _():
            src[pl.ds(inner_at, 2)] = left_in_ref[0]
            src[2 : panels + 2] = left_ref[0]
            src[pl.ds(outer_at, 2)] = left_out_ref[0]

        @pl.when(is_first == 0)
        def _():
            src[pl.ds(inner_at, 2)] = in_ref[...]
            src[2 : panels + 2] = mid_ref[...]
            src[pl.ds(outer_at, 2)] = out_ref[...]

        for column in range(2):
            for i in range(TERMS):
                wide[column, i] = jnp.broadcast_to(mix_ref[0, column, i : i + 1, :], (8, 128))

    def window(n):
        odd = jnp.clip(n - odd_first, 0, panels - 1) + panels + 4
        base = jnp.where(n < odd_first, jnp.minimum(n, panels + 1), odd)
        return src[pl.ds(base, 3)].reshape(BAND, LANES)

    def hand_out(n, res):
        slot = jnp.where((n >= 0) & (n < even_total), panels + 4 + n, dump)
        src[pl.ds(slot, 1)] = res[...][None]
        own_even = (n >= 1) & (n <= panels)
        own_odd = (n >= odd_first) & (n < odd_first + panels)
        to_keep = jnp.where(is_odd_home == 1, own_odd, own_even)
        to_send = jnp.where(is_odd_home == 1, own_even, own_odd)
        at_even = jnp.clip(n - 1, 0, panels - 1)
        at_odd = jnp.clip(n - odd_first, 0, panels - 1)
        at = jnp.where(own_odd, at_odd, at_even)

        @pl.when(to_keep)
        def _():
            keep_ref[pl.ds(at, 1)] = res[...][None]

        @pl.when(to_send)
        def _():
            send_ref[pl.ds(at, 1)] = res[...][None]

        @pl.when(own_odd)
        def _():
            pass_ref[pl.ds(at, 1)] = res[...][None]

    def phase(n):
        return (n >= odd_first).astype(jnp.int32)

    n = 2 * s

    @pl.when(s < count // 2)
    def _():
        dot_and_mix(ya, ca_ref, window(n), yb, wide, phase(n - 1), res_b)
        hand_out(n - 1, res_b)
        dot_and_mix(yb, cb_ref, window(n + 1), ya, wide, phase(n), res_a)
        hand_out(n, res_a)

    @pl.when(s == count // 2)
    def _():
        mix_rows(yb, wide, phase(n - 1), res_b, range(0, PAN, ROWS))
        hand_out(n - 1, res_b)


def one_turn(flags, left, inner, mid, outer, bands, mixing):
    panels = mid.shape[0]
    gap = 0 if panels >= 2 else 1
    odd_first = panels + 2 + gap
    count = odd_first + panels
    count += count % 2
    last = 2 * panels + 1

    def band_at(n):
        return jnp.minimum(jnp.where(n < odd_first, jnp.minimum(n, panels + 1), n - gap), last)

    block = jax.ShapeDtypeStruct((panels, PAN, LANES), jnp.bfloat16)
    whole = lambda shape: pl.BlockSpec(shape, lambda s, f: (0,) * len(shape))
    spec = pltpu.PrefetchScalarGridSpec(
        num_scalar_prefetch=1,
        grid=(count // 2 + 1,),
        in_specs=[
            pl.BlockSpec((1, 2, PAN, LANES), lambda s, f: (f[2], 0, 0, 0)),
            pl.BlockSpec((1, panels, PAN, LANES), lambda s, f: (f[2], 0, 0, 0)),
            pl.BlockSpec((1, 2, PAN, LANES), lambda s, f: (f[2], 0, 0, 0)),
            whole((2, PAN, LANES)),
            whole((panels, PAN, LANES)),
            whole((2, PAN, LANES)),
            pl.BlockSpec((1, STACK, BAND), lambda s, f: (band_at(2 * s), 0, 0)),
            pl.BlockSpec((1, STACK, BAND), lambda s, f: (band_at(2 * s + 1), 0, 0)),
            pl.BlockSpec((1, 2, TERMS, 128), lambda s, f: (f[2], 0, 0, 0)),
        ],
        out_specs=[whole((panels, PAN, LANES))] * 3,
        scratch_shapes=[
            pltpu.VMEM((2 * panels + 7, PAN, LANES), jnp.bfloat16),
            pltpu.VMEM((STACK, LANES), jnp.float32),
            pltpu.VMEM((STACK, LANES), jnp.float32),
            pltpu.VMEM((2, TERMS, 8, 128), jnp.float32),
            pltpu.VMEM((PAN, LANES), jnp.bfloat16),
            pltpu.VMEM((PAN, LANES), jnp.bfloat16),
        ],
    )
    steps = 2 * panels + 2
    return pl.pallas_call(
        functools.partial(turn_kernel, panels, odd_first, count),
        grid_spec=spec,
        out_shape=[block] * 3,
        compiler_params=pltpu.CompilerParams(vmem_limit_bytes=TURN_VMEM * MIB),
        cost_estimate=pl.CostEstimate(
            flops=steps * 2 * STACK * BAND * LANES * 2,
            bytes_accessed=steps * STACK * BAND * 2 * 3,
            transcendentals=0,
        ),
        name="two_columns",
    )(flags, *left, inner, mid, outer, bands, bands, mixing)


def pack_kernel(at_ref, left_ref, out_ref):
    low = lax.broadcasted_iota(jnp.int32, (PAN, 128), 1) < KB
    for q in range(PAIRS):
        even = left_ref[2 * q].astype(jnp.float32)
        odd = left_ref[2 * q + 1].astype(jnp.float32)
        first = jnp.where(low, even, pltpu.roll(odd, KB, 1))
        second = jnp.where(low, pltpu.roll(even, KB, 1), odd)
        out_ref[0, 0, :, q * 128 : (q + 1) * 128] = first.astype(jnp.bfloat16)
        out_ref[1, 0, :, q * 128 : (q + 1) * 128] = second.astype(jnp.bfloat16)


def packed(at, left, blocks):
    panels = left.shape[1] // PAN
    return pl.pallas_call(
        pack_kernel,
        grid_spec=pltpu.PrefetchScalarGridSpec(
            num_scalar_prefetch=1,
            grid=(blocks // 2, panels),
            in_specs=[pl.BlockSpec((D, PAN, 128), lambda c, p, f: (0, p, f[0] + c))],
            out_specs=pl.BlockSpec((2, 1, PAN, LANES), lambda c, p, f: (c, p, 0, 0)),
        ),
        out_shape=jax.ShapeDtypeStruct((blocks, panels, PAN, LANES), jnp.bfloat16),
        compiler_params=pltpu.CompilerParams(vmem_limit_bytes=32 * MIB),
        name="pack",
    )(at, left)


def unpack_kernel(at_ref, ka_ref, kb_ref, ga_ref, gb_ref, *rest):
    out_ref = rest[-1]
    low = lax.broadcasted_iota(jnp.int32, (PAN, 128), 1) < KB

    def unfold(one_ref, two_ref):
        for r in range(one_ref.shape[0]):
            rows = slice(r * PAN, (r + 1) * PAN)
            for q in range(PAIRS):
                lanes = slice(q * 128, (q + 1) * 128)
                one = one_ref[r, :, lanes].astype(jnp.float32)
                two = two_ref[r, :, lanes].astype(jnp.float32)
                first = jnp.where(low, one, pltpu.roll(two, KB, 1))
                second = jnp.where(low, pltpu.roll(one, KB, 1), two)
                out_ref[2 * q, rows, :] = first.astype(jnp.bfloat16)
                out_ref[2 * q + 1, rows, :] = second.astype(jnp.bfloat16)

    @pl.when(pl.program_id(0) == 0)
    def _():
        unfold(ka_ref, kb_ref)

    @pl.when(pl.program_id(0) == 1)
    def _():
        unfold(ga_ref, gb_ref)


def unpacked(at, held, shape, parts):
    panels = parts[0].shape[0]
    tall = 2 if panels % 2 == 0 else 1
    steps = panels // tall
    kept = pl.BlockSpec((tall, PAN, LANES), lambda s, p, f: (jnp.where(s == 0, p, steps - 1), 0, 0))
    got = pl.BlockSpec((tall, PAN, LANES), lambda s, p, f: (jnp.where(s == 0, 0, p), 0, 0))
    more = [] if held is None else [held]
    return pl.pallas_call(
        unpack_kernel,
        grid_spec=pltpu.PrefetchScalarGridSpec(
            num_scalar_prefetch=1,
            grid=(2, steps),
            in_specs=[kept] * 2 + [got] * 2 + [pl.BlockSpec(memory_space=pl.ANY)] * len(more),
            out_specs=pl.BlockSpec((D, tall * PAN, 128), lambda s, p, f: (0, p, f[s])),
        ),
        out_shape=jax.ShapeDtypeStruct(shape, jnp.bfloat16),
        input_output_aliases={5: 0} if more else {},
        compiler_params=pltpu.CompilerParams(vmem_limit_bytes=32 * MIB),
        name="unpack",
    )(at, *parts, *more)


def far_edges(block, width, dim):
    count = lax.axis_size("sec")
    have = block.shape[dim]
    low_parts, high_parts = [], []
    reach = 0
    while width > reach:
        hop = reach // have + 1
        take = min(have, width - reach)
        forward = [(i, i + hop) for i in range(count - hop)]
        backward = [(i + hop, i) for i in range(count - hop)]
        top = lax.slice_in_dim(block, have - take, have, axis=dim)
        bottom = lax.slice_in_dim(block, 0, take, axis=dim)
        low_parts.insert(0, lax.ppermute(top, "sec", forward))
        high_parts.append(lax.ppermute(bottom, "sec", backward))
        reach += take
    low, high = jnp.concatenate(low_parts, dim), jnp.concatenate(high_parts, dim)
    first = lax.axis_index("sec") % 2 == 0
    return jnp.where(first, high, low), jnp.where(first, low, high)


def side(block, width, dim, towards_inner):
    first = lax.axis_index("sec") % 2 == 0
    top_wanted = first if towards_inner else jnp.logical_not(first)
    start = jnp.where(top_wanted, block.shape[dim] - width, 0)
    return lax.dynamic_slice_in_dim(block, start, width, dim)


def inner_edge(block, width, dim=0):
    pairs = [(i, i ^ 1) for i in range(lax.axis_size("sec"))]
    return lax.ppermute(side(block, width, dim, True), "sec", pairs)


def outer_pairs():
    count = lax.axis_size("sec")
    forward = [(i, i + 1) for i in range(1, count - 1, 2)]
    return forward + [(j, i) for i, j in forward]


def both_edges(block, width, dim=0):
    if block.shape[dim] < width:
        return far_edges(block, width, dim)
    outer = lax.ppermute(side(block, width, dim, False), "sec", outer_pairs())
    return inner_edge(block, width, dim), outer


def on_device(left_start, coupling, tensor, sketch, block_parity, leg_parity):
    row_count, _, rank = left_start.shape
    panels = row_count // PAN
    col_count = lax.axis_size("col")
    sec_count = lax.axis_size("sec")
    col_index = lax.axis_index("col")
    sec_index = lax.axis_index("sec")
    stage = col_index // 2
    half = col_index % 2
    stages = col_count // 2
    half_cols = rank // 2
    blocks = half_cols // KB
    swap = [(i, i ^ 1) for i in range(col_count)]
    up = [(i, i + 2) for i in range(col_count - 2)]

    legs = lax.dynamic_index_in_dim(leg_parity, col_index, 0, keepdims=False)
    parity = lax.dynamic_slice_in_dim(
        jnp.pad(block_parity, (1, 1)), sec_index * panels, panels + 2, 0
    )
    table = 1.0 - 2.0 * (parity[:, None] * legs[None, :]).astype(jnp.float32)
    signs = jnp.stack([table[w : w + panels] for w in range(3)], 1).reshape(panels, 3 * D)
    own = ordered_coupling(coupling[0], signs)
    odd_home = half == 1
    rim = jnp.concatenate([own[:1], own[panels - 1 :]], 0) if panels > 1 else own
    other_rim = lax.ppermute(rim, "col", swap)
    own_inner, own_outer = both_edges(rim, 1)

    tensor, sketch, rim = lax.optimization_barrier((tensor, sketch, rim))
    small = jnp.concatenate([tensor[0].reshape(D, D * D * D), sketch[0]], 1)
    small_other = lax.ppermute(small, "col", swap)

    def mixing_of(both):
        legs_part = both[:, : D * D * D].reshape(D, D, D, D)
        cols = lax.dynamic_slice_in_dim(both, D * D * D + half * half_cols, half_cols, 1)
        m = jnp.einsum("duez,zk->duek", legs_part, cols, precision=lax.Precision.HIGHEST)
        m = m.reshape(PAIRS, 2, D, D, blocks, KB).transpose(4, 2, 0, 3, 1, 5)
        return m.reshape(blocks, TERMS, 2 * KB)

    mixing = jnp.stack(
        [
            mixing_of(jnp.where(odd_home, small_other, small)),
            mixing_of(jnp.where(odd_home, small, small_other)),
        ],
        1,
    )

    at_half = (half * (blocks // 2)).astype(jnp.int32)[None]
    mine = packed(at_half, left_start.transpose(1, 0, 2), blocks)
    left_inner, left_outer = both_edges(mine, 2, 1)

    if panels > 2:
        inner = own[1 : panels - 1]
        other_inner = lax.ppermute(inner, "col", swap)
        other = [other_rim[:1], other_inner, other_rim[1:]]
        mine_too = [own[:1], own[1 : panels - 1], own[panels - 1 :]]
    else:
        other, mine_too = [other_rim], [own]
    other_rim, mixing, mine = lax.optimization_barrier((other_rim, mixing, mine))
    other_inner_edge, other_outer_edge = both_edges(other_rim, 1)
    even_inner = jnp.where(odd_home, other_inner_edge, own_inner)
    even_outer = jnp.where(odd_home, other_outer_edge, own_outer)
    first_core = sec_index % 2 == 0
    even_low = jnp.where(first_core, even_outer, even_inner)
    even_high = jnp.where(first_core, even_inner, even_outer)
    even_bands = [
        jnp.where(odd_home, b, a)
        for a, b in zip(mine_too, other)
    ]
    odd_bands = [jnp.where(odd_home, a, b) for a, b in zip(mine_too, other)]
    even_bands = [even_low] + even_bands + [even_high]
    left_inner, left_outer, mixing, *rest = lax.optimization_barrier(
        (left_inner, left_outer, mixing, *even_bands, *odd_bands)
    )
    bands = jnp.concatenate(rest, 0)
    left = (left_inner, mine, left_outer)

    skew = SKEW
    turns = blocks + skew * (stages - 1)
    zero_edge = jnp.zeros((2, PAN, LANES), jnp.bfloat16)
    zero_mid = jnp.zeros((panels, PAN, LANES), jnp.bfloat16)
    arrived = {t: (zero_edge, zero_mid, zero_edge) for t in range(skew)}
    keeps, sends = {}, {}
    kept = []
    lag = skew * (stages - 1)

    def staged(table_of, i):
        out = table_of[i + lag]
        for z in range(stages - 1):
            out = jnp.where(stage == z, table_of[i + skew * z], out)
        return out

    flying, swapping = {}, {}
    states = None
    across = [
        (c * sec_count + i, (c + 2) * sec_count + j)
        for c in range(col_count - 2)
        for i, j in outer_pairs()
    ]
    direct = panels >= 2
    for t in range(turns):
        index = jnp.clip(t - skew * stage, 0, blocks - 1)
        flags = jnp.stack([half, (stage == 0).astype(jnp.int32), index, sec_index % 2])
        flags = flags.astype(jnp.int32)
        inner, mid, outer = arrived.pop(t)
        if t - 2 in swapping:
            flags, swapping[t - 2] = lax.optimization_barrier((flags, swapping[t - 2]))
        keeps[t], sends[t], passed = one_turn(flags, left, inner, mid, outer, bands, mixing)
        if t - 1 in flying:
            (nxt, outer), passed = lax.optimization_barrier((flying[t - 1], passed))
            if direct:
                inner = inner_edge(nxt, 2)
            else:
                inner, outer = far_edges(nxt, 2, 0)
            arrived[t - 1 + skew] = (inner, nxt, outer)
        if t + skew < turns:
            nxt = lax.ppermute(passed, "col", up)
            edge = nxt
            if direct:
                edge = lax.ppermute(side(passed, 2, 0, False), ("col", "sec"), across)
            flying[t] = (nxt, edge)
        if t >= lag:
            i = t - lag
            swapping[t] = lax.ppermute(staged(sends, i), "col", swap)
            kept.append(staged(keeps, i))
        for j in range(1, blocks, 2):
            if t == j + lag + 2 or (t == turns - 1 and j + lag + 2 > t):
                at = jnp.stack([half, 1 - half]) * (blocks // 2) + j // 2
                parts = (kept[j - 1], kept[j], swapping[j - 1 + lag], swapping[j + lag])
                states = unpacked(at.astype(jnp.int32), states, (D, row_count, rank), parts)

    flat = states.reshape(D * row_count, rank)
    share = rank // sec_count
    group = sec_count // 2
    top = sec_index // group
    halves = {}
    for name, which in (("far", 1 - top), ("near", top)):
        columns = lax.dynamic_slice_in_dim(flat, which * (rank // 2), rank // 2, 1)
        if name == "near":
            columns, far_now = lax.optimization_barrier((columns, halves["far"]))
            halves["far"] = far_now
            crossed = lax.ppermute(far_now, "sec", [(i, i ^ group) for i in range(sec_count)])
        gram = lax.dot_general(
            columns, flat, (((0,), (0,)), ((), ())), preferred_element_type=jnp.float32
        ).astype(jnp.bfloat16)
        gram = gram.reshape(group, share, rank)
        width = 1
        while width < group:
            bit = (sec_index // width) % 2
            pairs = gram.reshape(-1, 2, share, rank)
            stay = lax.dynamic_index_in_dim(pairs, bit, 1, keepdims=False)
            away = lax.dynamic_index_in_dim(pairs, 1 - bit, 1, keepdims=False)
            come = lax.ppermute(away, "sec", [(i, i ^ width) for i in range(sec_count)])
            gram = stay.astype(jnp.float32) + come.astype(jnp.float32)
            if name == "far" or gram.shape[0] > 1:
                gram = gram.astype(jnp.bfloat16)
            width *= 2
        halves[name] = gram
    gram_out = (halves["near"].astype(jnp.float32) + crossed.astype(jnp.float32)) * (1.0 / (CHI * D))
    return states.transpose(1, 0, 2)[None], gram_out


def solution(mesh):
    in_specs = (
        P("sec", None, None),
        P("col", "sec", None),
        P("col", None, None, None, None),
        P("col", None, None),
        P(),
        P(),
    )
    out_specs = (P("col", "sec", None, None), P("col", "sec", None))
    return jax.shard_map(
        on_device, mesh=mesh, in_specs=in_specs, out_specs=out_specs, check_vma=False
    )
```
